32 devices in a mesh: row: 4 (over z), col: 8 (over y, x, core).
Axes of the slice: x: 2, y: 2, z: 4, core: 2. Of those that a mesh axis runs over, the one named last changes fastest.
Arguments:
- inputs: bfloat16 [512, 8192], P(None, 'row'), may hold values from -6 to 6
- up_weight: bfloat16 [8192, 28672], P('row', 'col'), may hold values from -0.109375 to 0.109375
- down_weight: bfloat16 [28672, 8192], P('col', 'row'), may hold values from -0.0546875 to 0.0546875
- up_mask: int32 [64, 224], P('row', 'col'), may hold values 0 or 1
- down_mask: int32 [224, 64], P('col', 'row'), may hold values 0 or 1
- cotangent: bfloat16 [512, 8192], P(None, 'row'), may hold values from -6 to 6
Outputs:
- output: bfloat16 [512, 8192], P(None, 'row')
- input_grad: bfloat16 [512, 8192], P(None, 'row')
- up_grad: bfloat16 [8192, 28672], P('row', 'col')
- down_grad: bfloat16 [28672, 8192], P('col', 'row')
The draws below stay inside these ranges and needn't reach their ends.
All inputs are finite; a program needn't handle non-finite values. No bound on the sum of `up_mask` or of `down_mask` on one device may be relied on, other than what follows from the above.
Results may differ from the reference program's by a relative error of at most 0.0051.
Values may be sent and summed in bfloat16 or wider, within the bound.
A program may use at most 128 MiB of HBM per device.

```python
import jax
import jax.numpy as jnp

D = 8192
FF = 28672
BLK = 128
TOKENS = 512


def touch_ends(drawn, rng, smallest, top_value):
    shape = drawn.shape
    spot = [jax.random.randint(jax.random.fold_in(rng, axis), (), 0, shape[axis]) for axis in range(len(shape))]
    drawn = drawn.at[tuple(spot)].set(smallest)
    longest = shape.index(max(shape))
    spot[longest] = (spot[longest] + 1) % shape[longest]
    return drawn.at[tuple(spot)].set(top_value)


def shard_levels(key, dims, shards, smallest, top_value):
    factor_of, own = 1.0, jax.random.fold_in(key, 6)
    for dim, blocks in shards:
        heights = jnp.exp(jax.random.uniform(jax.random.fold_in(own, dim), (blocks,), jnp.float32, smallest / len(shards), top_value / len(shards)))
        factor_of = factor_of * jnp.repeat(heights, dims[dim] // blocks).reshape([-1 if axis == dim else 1 for axis in range(len(dims))])
    return factor_of


def centred(key, shape, spread, most, shards=(), dtype=jnp.bfloat16):
    values = jax.random.normal(key, shape, jnp.float32) * spread
    if len(shards) > 0:
        values = shard_levels(key, shape, shards, -0.22, 0.18) * values
    return jnp.clip(values, min=-most, max=most).astype(dtype)


def setup_inputs(seed: int = 0) -> dict:
    arg_keys = jax.random.split(jax.random.key(seed), 7)
    return {
        "inputs": centred(arg_keys[0], (TOKENS, D), 1.0, 6.0, ((1, 4),)),
        "up_weight": centred(arg_keys[1], (D, FF), (D * 2 // 5) ** -0.5, 0.109375, ((0, 4), (1, 8))),
        "down_weight": centred(arg_keys[2], (FF, D), (FF * 2 // 5) ** -0.5, 0.0546875, ((0, 8), (1, 4))),
        "up_mask": touch_ends((jax.random.randint(arg_keys[3], (D // BLK, FF // BLK), 0, 5) < 2).astype(jnp.int32), jax.random.fold_in(arg_keys[3], 1), 0, 1),
        "down_mask": touch_ends((jax.random.randint(arg_keys[4], (FF // BLK, D // BLK), 0, 5) < 2).astype(jnp.int32), jax.random.fold_in(arg_keys[4], 1), 0, 1),
        "cotangent": centred(arg_keys[5], (TOKENS, D), 1.0, 6.0, ((1, 4),)),
    }


def expand(mask, block):
    kept = mask > 0
    return jnp.repeat(jnp.repeat(kept, block, axis=0), block, axis=1)

def activate(value):
    return jax.nn.gelu(value, approximate=True)

def reference(inputs, up_weight, down_weight, up_mask, down_mask, cotangent):
    block = up_weight.shape[0] // up_mask.shape[0]
    keep_up = expand(up_mask, block)
    keep_down = expand(down_mask, block)
    masked_up = jnp.where(keep_up, up_weight, jnp.zeros_like(up_weight))
    masked_down = jnp.where(keep_down, down_weight, jnp.zeros_like(down_weight))
    hidden = jnp.dot(inputs, masked_up, preferred_element_type=jnp.float32)
    active_full, pull_back = jax.vjp(activate, hidden)
    active = active_full.astype(jnp.bfloat16)
    output = jnp.dot(active, masked_down, preferred_element_type=jnp.float32).astype(jnp.bfloat16)
    active_grad = jnp.dot(cotangent, masked_down.T, preferred_element_type=jnp.float32)
    hidden_grad = pull_back(active_grad)[0].astype(jnp.bfloat16)
    input_grad = jnp.dot(hidden_grad, masked_up.T, preferred_element_type=jnp.float32).astype(jnp.bfloat16)
    up_full = jnp.dot(inputs.T, hidden_grad, preferred_element_type=jnp.float32)
    up_grad = jnp.where(keep_up, up_full, jnp.zeros_like(up_full)).astype(jnp.bfloat16)
    down_full = jnp.dot(active.T, cotangent, preferred_element_type=jnp.float32)
    down_grad = jnp.where(keep_down, down_full, jnp.zeros_like(down_full)).astype(jnp.bfloat16)
    return (output, input_grad, up_grad, down_grad)
```

```python
import functools

import jax
import jax.numpy as jnp
from jax import lax
from jax.experimental import pallas as pl
from jax.experimental.pallas import tpu as pltpu
from jax.sharding import PartitionSpec as P

MESH = pl.DeviceIdType.MESH
F32 = jnp.float32
BF16 = jnp.bfloat16
SLOTS = 6
DEFER = 2
LIMIT = 63 * 1024 * 1024
NT = (((1,), (1,)), ((), ()))
TN = (((0,), (0,)), ((), ()))
ROOT = 0.7978845608028654
CUBE = 0.044715


def gelu_and_slope(v):
    square = v * v
    tanh = jnp.tanh(ROOT * v * (1.0 + CUBE * square))
    half = 0.5 * (1.0 + tanh)
    slope = half + 0.5 * v * (1.0 - tanh * tanh) * (ROOT * (1.0 + 3.0 * CUBE * square))
    return v * half, slope


def layer_kernel(
    rows, cols, halves, width, block,
    x, ct, up_hbm, dn_hbm, keep_up, keep_dn,
    sums, act_hbm, hg_hbm,
    up_v, dn_v, acc, to_inner, from_outer, from_inner,
    pair_out, pair_in, half, chip_in, fin,
    w_sem, in_send, out_recv, in_recv, out_send, store_sem, cred_in, cred_out,
    s0, r0, s1, r1, s2, r2, s3, r3, own_sem,
):
    tokens, d_model = x.shape
    chunks = up_v.shape[0]
    tm = tokens // halves
    steps = halves * chunks
    chips = cols // 2
    part = tm // cols
    me_r, me_c = lax.axis_index("row"), lax.axis_index("col")
    chip, core = lax.div(me_c, 2), lax.rem(me_c, 2)
    sibling = (me_r, chip * 2 + 1 - core)
    mid = rows // 2
    left = me_r < mid
    toward = jnp.where(left, 1, -1)
    dist = jnp.where(left, mid - 1 - me_r, me_r - mid)
    is_mid = dist == 0
    has_outer = jnp.logical_and(me_r > 0, me_r < rows - 1)
    inner = (me_r + toward, me_c)
    outer = (lax.rem(me_r - toward + rows, rows), me_c)
    lag = 2 + 3 * dist

    def chip_peer(j):
        return (me_r, lax.rem(chip + j, chips) * 2 + core)

    def weight_copies(c):
        at = pl.multiple_of(c * width, width)
        return (
            pltpu.make_async_copy(up_hbm.at[:, pl.ds(at, width)], up_v.at[c], w_sem.at[0, c]),
            pltpu.make_async_copy(dn_hbm.at[pl.ds(at, width), :], dn_v.at[c], w_sem.at[1, c]),
        )

    @pl.loop(0, chunks)
    def _(c):
        for copy in weight_copies(c):
            copy.start()

    barrier = pltpu.get_barrier_semaphore()
    greet = [inner, sibling] + [chip_peer(j) for j in range(1, chips)]
    for device in greet:
        pl.semaphore_signal(barrier, inc=1, device_id=device, device_id_type=MESH)

    @pl.when(has_outer)
    def _():
        pl.semaphore_signal(barrier, inc=1, device_id=outer, device_id_type=MESH)

    for t in range(halves):
        for which in range(2):
            acc[t, which] = jnp.zeros((tm, d_model), F32)

    @pl.when(has_outer)
    def _():
        pl.semaphore_wait(barrier, len(greet) + 1)

    @pl.when(jnp.logical_not(has_outer))
    def _():
        pl.semaphore_wait(barrier, len(greet))

    def inward(k, middle):
        return pltpu.make_async_remote_copy(
            src_ref=to_inner.at[k],
            dst_ref=from_inner.at[k] if middle else from_outer.at[k],
            send_sem=in_send.at[k],
            recv_sem=in_recv.at[k] if middle else out_recv.at[k],
            device_id=inner,
            device_id_type=MESH,
        )

    def outward(k):
        return pltpu.make_async_remote_copy(
            src_ref=from_inner.at[k],
            dst_ref=from_inner.at[k],
            send_sem=out_send.at[k],
            recv_sem=in_recv.at[k],
            device_id=outer,
            device_id_type=MESH,
        )

    def stores(u):
        k = lax.rem(u, SLOTS)
        row = pl.multiple_of(lax.div(u, chunks) * tm, tm)
        col = pl.multiple_of(lax.rem(u, chunks) * width, width)
        there = (pl.ds(row, tm), pl.ds(col, width))
        return (
            pltpu.make_async_copy(from_inner.at[k, 0], act_hbm.at[there], store_sem.at[0, k]),
            pltpu.make_async_copy(from_inner.at[k, 1], hg_hbm.at[there], store_sem.at[1, k]),
        )

    def apply_mask(c):
        per = width // block

        @pl.loop(0, d_model // block)
        def _(b):
            at = pl.ds(pl.multiple_of(b * block, block), block)
            for j in range(per):
                lanes = pl.ds(j * block, block)
                keep = keep_up[b, c * per + j]
                up_v[c, at, lanes] = (up_v[c, at, lanes].astype(F32) * keep).astype(BF16)
                keep = keep_dn[c * per + j, b]
                dn_v[c, lanes, at] = (dn_v[c, lanes, at].astype(F32) * keep).astype(BF16)

    def produce(s):
        t, c, k = lax.div(s, chunks), lax.rem(s, chunks), lax.rem(s, SLOTS)

        @pl.when(t == 0)
        def _():
            for copy in weight_copies(c):
                copy.wait()
            apply_mask(c)

        token = pl.ds(pl.multiple_of(t * tm, tm), tm)
        h = jnp.dot(x[token, :], up_v[c], preferred_element_type=F32)
        g = lax.dot_general(ct[token, :], dn_v[c], NT, preferred_element_type=F32)

        @pl.when(s >= SLOTS)
        def _():
            inward(k, True).wait_send()
            pl.semaphore_wait(cred_in, 1)

        @pl.when(has_outer)
        def _():
            outward_in(k).wait_recv()
            to_inner[k, 0] = (h + from_outer[k, 0].astype(F32)).astype(BF16)
            to_inner[k, 1] = (g + from_outer[k, 1].astype(F32)).astype(BF16)

            @pl.when(s + SLOTS < steps)
            def _():
                pl.semaphore_signal(cred_in, inc=1, device_id=outer, device_id_type=MESH)

        @pl.when(jnp.logical_not(has_outer))
        def _():
            to_inner[k, 0] = h.astype(BF16)
            to_inner[k, 1] = g.astype(BF16)

        @pl.when(is_mid)
        def _():
            inward(k, True).start()

        @pl.when(jnp.logical_not(is_mid))
        def _():
            inward(k, False).start()

    def outward_in(k):
        return inward(k, False)

    def release(u):
        k = lax.rem(u, SLOTS)
        for copy in stores(u):
            copy.wait()

        @pl.when(has_outer)
        def _():
            outward(k).wait_send()

        @pl.when(u + SLOTS < steps)
        def _():
            @pl.when(is_mid)
            def _():
                pl.semaphore_signal(cred_in, inc=1, device_id=inner, device_id_type=MESH)

            @pl.when(jnp.logical_not(is_mid))
            def _():
                pl.semaphore_signal(cred_out, inc=1, device_id=inner, device_id_type=MESH)

    def consume(u):
        t, c, k = lax.div(u, chunks), lax.rem(u, chunks), lax.rem(u, SLOTS)
        outward(k).wait_recv()

        @pl.when(is_mid)
        def _():
            h = to_inner[k, 0].astype(F32) + from_inner[k, 0].astype(F32)
            g = to_inner[k, 1].astype(F32) + from_inner[k, 1].astype(F32)
            active, slope = gelu_and_slope(h)
            from_inner[k, 0] = active.astype(BF16)
            from_inner[k, 1] = (g * slope).astype(BF16)

        @pl.when(has_outer)
        def _():
            @pl.when(u >= SLOTS)
            def _():
                pl.semaphore_wait(cred_out, 1)

            outward(k).start()

        for copy in stores(u):
            copy.start()
        acc[t, 0] += jnp.dot(from_inner[k, 0], dn_v[c], preferred_element_type=F32)
        acc[t, 1] += lax.dot_general(from_inner[k, 1], up_v[c], NT, preferred_element_type=F32)

        @pl.when(u >= DEFER)
        def _():
            release(u - DEFER)

    def rows_of(t, owner, first, count):
        return pl.ds(pl.multiple_of(t * tm + owner * (tm // 2) + first, part), count)

    def pair_copy(t):
        return pltpu.make_async_remote_copy(
            src_ref=pair_out.at[t], dst_ref=pair_in.at[t], send_sem=s0.at[t], recv_sem=r0.at[t],
            device_id=sibling, device_id_type=MESH)

    def chip_copy(t, j):
        return pltpu.make_async_remote_copy(
            src_ref=half.at[t, lax.rem(chip + j, chips)], dst_ref=chip_in.at[t, j - 1],
            send_sem=s1.at[t, j - 1], recv_sem=r1.at[t, j - 1],
            device_id=chip_peer(j), device_id_type=MESH)

    def spread_copy(t, j):
        mine = rows_of(t, core, chip * part, part)
        return pltpu.make_async_remote_copy(
            src_ref=fin.at[t], dst_ref=sums.at[:, mine, :],
            send_sem=s2.at[t, j - 1], recv_sem=r2.at[t, j - 1],
            device_id=chip_peer(j), device_id_type=MESH)

    def own_copy(t):
        mine = rows_of(t, core, chip * part, part)
        return pltpu.make_async_copy(fin.at[t], sums.at[:, mine, :], own_sem.at[t])

    def share_copy(t):
        mine = rows_of(t, core, 0, tm // 2)
        return pltpu.make_async_remote_copy(
            src_ref=sums.at[:, mine, :], dst_ref=sums.at[:, mine, :], send_sem=s3.at[t], recv_sem=r3.at[t],
            device_id=sibling, device_id_type=MESH)

    def phase0(t):
        other = pl.ds(pl.multiple_of((1 - core) * (tm // 2), tm // 2), tm // 2)
        for which in range(2):
            pair_out[t, which] = acc[t, which, other, :].astype(BF16)
        pair_copy(t).start()

    def phase1(t):
        pair_copy(t).wait()

        @pl.loop(0, chips)
        def _(q):
            mine = pl.ds(pl.multiple_of(core * (tm // 2) + q * part, part), part)
            there = pl.ds(pl.multiple_of(q * part, part), part)
            for which in range(2):
                half[t, q, which] = (acc[t, which, mine, :] + pair_in[t, which, there, :].astype(F32)).astype(BF16)

        for j in range(1, chips):
            chip_copy(t, j).start()

    def phase2(t):
        for j in range(1, chips):
            chip_copy(t, j).wait()
        for which in range(2):
            total = half[t, chip, which].astype(F32)
            for j in range(1, chips):
                total = total + chip_in[t, j - 1, which].astype(F32)
            fin[t, which] = total.astype(BF16)
        own_copy(t).start()
        for j in range(1, chips):
            spread_copy(t, j).start()

    def phase3(t):
        own_copy(t).wait()
        for j in range(1, chips):
            spread_copy(t, j).wait()
        share_copy(t).start()

    def phase4(t):
        share_copy(t).wait()

    phases = ((0, phase0), (2, phase1), (4, phase2), (6, phase3))
    late = []

    @pl.loop(0, steps + lag)
    def _(s):
        @pl.when(s < steps)
        def _():
            produce(s)

        @pl.when(s >= lag)
        def _():
            u = s - lag
            consume(u)
            for t in range(halves):
                for after, phase in phases:
                    at = (t + 1) * chunks - 1 + after
                    if at < steps:
                        @pl.when(u == at)
                        def _(phase=phase, t=t):
                            phase(t)

    for t in range(halves):
        for after, phase in phases:
            if (t + 1) * chunks - 1 + after >= steps:
                phase(t)
    for u in range(steps - DEFER, steps):
        release(u)

    @pl.loop(steps - SLOTS, steps)
    def _(s):
        inward(lax.rem(s, SLOTS), True).wait_send()

    for t in range(halves):
        phase4(t)


def grads_kernel(block, x, ct, act, hg, keep_up, keep_dn, up_out, dn_out, xt):
    c = pl.program_id(0)
    width = hg.shape[1]
    per = width // block

    @pl.when(c == 0)
    def _():
        xt[...] = x[...].T

    @pl.loop(0, xt.shape[0] // block // 2)
    def _(pair):
        at = pl.ds(pl.multiple_of(pair * 2 * block, 2 * block), 2 * block)
        full = jnp.dot(xt[at, :], hg[...], preferred_element_type=F32)
        for i in range(2):
            for j in range(per):
                lanes = slice(j * block, (j + 1) * block)
                keep = keep_up[pair * 2 + i, c * per + j]
                there = pl.ds(pl.multiple_of((pair * 2 + i) * block, block), block)
                up_out[there, lanes] = (full[i * block:(i + 1) * block, lanes] * keep).astype(BF16)

    at_t = act[...].T

    @pl.loop(0, ct.shape[1] // block // 2)
    def _(pair):
        at = pl.ds(pl.multiple_of(pair * 2 * block, 2 * block), 2 * block)
        full = jnp.dot(at_t, ct[:, at], preferred_element_type=F32)
        for i in range(2):
            there = pl.ds(pl.multiple_of((pair * 2 + i) * block, block), block)
            for j in range(per):
                lanes = slice(j * block, (j + 1) * block)
                keep = keep_dn[c * per + j, pair * 2 + i]
                dn_out[lanes, there] = (full[lanes, i * block:(i + 1) * block] * keep).astype(BF16)


def body(rows, cols, inputs, up_weight, down_weight, up_mask, down_mask, cotangent):
    tokens, d_model = inputs.shape
    hidden = up_weight.shape[1]
    block = d_model // up_mask.shape[0]
    keep_up = (up_mask > 0).astype(F32)
    keep_dn = (down_mask > 0).astype(F32)
    width = 2 * block if hidden % (2 * block) == 0 else block
    chunks = hidden // width
    halves = 2
    tm = tokens // halves
    chips = cols // 2
    part = tm // cols
    vmem = pl.BlockSpec(memory_space=pltpu.VMEM)
    smem = pl.BlockSpec(memory_space=pltpu.SMEM)
    hbm = pl.BlockSpec(memory_space=pl.ANY)
    dma = pltpu.SemaphoreType.DMA
    sums, act, hg = pl.pallas_call(
        functools.partial(layer_kernel, rows, cols, halves, width, block),
        out_shape=(
            jax.ShapeDtypeStruct((2, tokens, d_model), BF16),
            jax.ShapeDtypeStruct((tokens, hidden), BF16),
            jax.ShapeDtypeStruct((tokens, hidden), BF16),
        ),
        in_specs=[vmem, vmem, hbm, hbm, smem, smem],
        out_specs=(hbm, hbm, hbm),
        scratch_shapes=[
            pltpu.VMEM((chunks, d_model, width), BF16),
            pltpu.VMEM((chunks, width, d_model), BF16),
            pltpu.VMEM((halves, 2, tm, d_model), F32),
            pltpu.VMEM((SLOTS, 2, tm, width), BF16),
            pltpu.VMEM((SLOTS, 2, tm, width), BF16),
            pltpu.VMEM((SLOTS, 2, tm, width), BF16),
            pltpu.VMEM((halves, 2, tm // 2, d_model), BF16),
            pltpu.VMEM((halves, 2, tm // 2, d_model), BF16),
            pltpu.VMEM((halves, chips, 2, part, d_model), BF16),
            pltpu.VMEM((halves, max(chips - 1, 1), 2, part, d_model), BF16),
            pltpu.VMEM((halves, 2, part, d_model), BF16),
            dma((2, chunks)),
            dma((SLOTS,)), dma((SLOTS,)), dma((SLOTS,)), dma((SLOTS,)),
            dma((2, SLOTS)),
            pltpu.SemaphoreType.REGULAR, pltpu.SemaphoreType.REGULAR,
            dma((halves,)), dma((halves,)),
            dma((halves, max(chips - 1, 1))), dma((halves, max(chips - 1, 1))),
            dma((halves, max(chips - 1, 1))), dma((halves, max(chips - 1, 1))),
            dma((halves,)), dma((halves,)),
            dma((halves,)),
        ],
        compiler_params=pltpu.CompilerParams(collective_id=0, has_side_effects=True, vmem_limit_bytes=LIMIT),
        cost_estimate=pl.CostEstimate(
            flops=8 * tokens * d_model * hidden, bytes_accessed=4 * d_model * hidden, transcendentals=tokens * hidden),
    )(inputs, cotangent, up_weight, down_weight, keep_up, keep_dn)

    wide = next(w for w in (4 * block, 2 * block, block) if hidden % w == 0)
    up_grad, down_grad = pl.pallas_call(
        functools.partial(grads_kernel, block),
        grid=(hidden // wide,),
        out_shape=(
            jax.ShapeDtypeStruct((d_model, hidden), BF16),
            jax.ShapeDtypeStruct((hidden, d_model), BF16),
        ),
        in_specs=[
            pl.BlockSpec((tokens, d_model), lambda c: (0, 0)),
            pl.BlockSpec((tokens, d_model), lambda c: (0, 0)),
            pl.BlockSpec((tokens, wide), lambda c: (0, c)),
            pl.BlockSpec((tokens, wide), lambda c: (0, c)),
            smem, smem,
        ],
        out_specs=(
            pl.BlockSpec((d_model, wide), lambda c: (0, c)),
            pl.BlockSpec((wide, d_model), lambda c: (c, 0)),
        ),
        scratch_shapes=[pltpu.VMEM((d_model, tokens), BF16)],
        compiler_params=pltpu.CompilerParams(vmem_limit_bytes=48 * 1024 * 1024),
        cost_estimate=pl.CostEstimate(
            flops=4 * tokens * d_model * hidden, bytes_accessed=4 * d_model * hidden, transcendentals=0),
    )(inputs, cotangent, act, hg, keep_up, keep_dn)
    return (sums[0], sums[1], up_grad, down_grad)


def solution(mesh):
    in_specs = (
        P(None, "row"),
        P("row", "col"),
        P("col", "row"),
        P("row", "col"),
        P("col", "row"),
        P(None, "row"),
    )
    out_specs = (P(None, "row"), P(None, "row"), P("row", "col"), P("col", "row"))
    step = functools.partial(body, mesh.shape["row"], mesh.shape["col"])
    return jax.shard_map(step, mesh=mesh, in_specs=in_specs, out_specs=out_specs, check_vma=False)
```

```python
import functools

import jax
import jax.numpy as jnp
from jax import lax
from jax.experimental import pallas as pl
from jax.experimental.pallas import tpu as pltpu
from jax.sharding import PartitionSpec as P

MESH = pl.DeviceIdType.MESH
F32 = jnp.float32
BF16 = jnp.bfloat16
DEFER = 2
LIMIT = 63 * 1024 * 1024
NT = (((1,), (1,)), ((), ()))
TN = (((0,), (0,)), ((), ()))
ROOT = 0.7978845608028654
CUBE = 0.044715


def gelu_and_slope(v):
    square = v * v
    tanh = jnp.tanh(ROOT * v * (1.0 + CUBE * square))
    half = 0.5 * (1.0 + tanh)
    slope = half + 0.5 * v * (1.0 - tanh * tanh) * (ROOT * (1.0 + 3.0 * CUBE * square))
    return v * half, slope


def splat(keep, block):
    tile = jnp.full((16, block), keep.astype(F32)).astype(BF16)
    return jnp.broadcast_to(tile[None], (block // 16, 16, block)).reshape(block, block)


def layer_kernel(
    rows, cols, halves, width, block, slots,
    x, ct, up_hbm, dn_hbm, keep_up, keep_dn,
    sums, act_hbm, hg_hbm,
    up_v, dn_v, acc, to_inner, from_outer, from_inner, turned,
    pair_out, pair_in, half, chip_in, fin,
    w_sem, in_send, out_recv, in_recv, out_send, store_sem, cred_in, cred_out,
    s0, r0, s1, r1, s2, r2, s3, r3, own_sem,
):
    tokens, d_model = x.shape
    chunks = up_v.shape[0]
    tm = tokens // halves
    steps = halves * chunks
    chips = cols // 2
    part = tm // cols
    me_r, me_c = lax.axis_index("row"), lax.axis_index("col")
    chip, core = lax.div(me_c, 2), lax.rem(me_c, 2)
    sibling = (me_r, chip * 2 + 1 - core)
    mid = rows // 2
    left = me_r < mid
    toward = jnp.where(left, 1, -1)
    dist = jnp.where(left, mid - 1 - me_r, me_r - mid)
    is_mid = dist == 0
    has_outer = jnp.logical_and(me_r > 0, me_r < rows - 1)
    inner = (me_r + toward, me_c)
    outer = (lax.rem(me_r - toward + rows, rows), me_c)
    lag = 2 + 3 * dist

    def chip_peer(j):
        return (me_r, lax.rem(chip + j, chips) * 2 + core)

    def weight_copies(c):
        at = pl.multiple_of(c * width, width)
        return (
            pltpu.make_async_copy(up_hbm.at[:, pl.ds(at, width)], up_v.at[c], w_sem.at[0, c]),
            pltpu.make_async_copy(dn_hbm.at[pl.ds(at, width), :], dn_v.at[c], w_sem.at[1, c]),
        )

    @pl.loop(0, chunks)
    def _(c):
        for copy in weight_copies(c):
            copy.start()

    barrier = pltpu.get_barrier_semaphore()
    greet = [inner, sibling] + [chip_peer(j) for j in range(1, chips)]
    for device in greet:
        pl.semaphore_signal(barrier, inc=1, device_id=device, device_id_type=MESH)

    @pl.when(has_outer)
    def _():
        pl.semaphore_signal(barrier, inc=1, device_id=outer, device_id_type=MESH)

    for t in range(halves):
        for which in range(2):
            acc[t, which] = jnp.zeros((tm, d_model), F32)

    @pl.when(has_outer)
    def _():
        pl.semaphore_wait(barrier, len(greet) + 1)

    @pl.when(jnp.logical_not(has_outer))
    def _():
        pl.semaphore_wait(barrier, len(greet))

    def inward(k, middle):
        return pltpu.make_async_remote_copy(
            src_ref=to_inner.at[k],
            dst_ref=from_inner.at[k] if middle else from_outer.at[k],
            send_sem=in_send.at[k],
            recv_sem=in_recv.at[k] if middle else out_recv.at[k],
            device_id=inner,
            device_id_type=MESH,
        )

    def outward(k):
        return pltpu.make_async_remote_copy(
            src_ref=from_inner.at[k],
            dst_ref=from_inner.at[k],
            send_sem=out_send.at[k],
            recv_sem=in_recv.at[k],
            device_id=outer,
            device_id_type=MESH,
        )

    def stores(u):
        k = lax.rem(u, slots)
        row = pl.multiple_of(lax.div(u, chunks) * tm, tm)
        col = pl.multiple_of(lax.rem(u, chunks) * width, width)
        token, unit = pl.ds(row, tm), pl.ds(col, width)
        return (
            pltpu.make_async_copy(turned.at[k], act_hbm.at[unit, token], store_sem.at[0, k]),
            pltpu.make_async_copy(from_inner.at[k, 1], hg_hbm.at[token, unit], store_sem.at[1, k]),
        )

    def apply_mask(c):
        per = width // block

        @pl.loop(0, d_model // block)
        def _(b):
            at = pl.ds(pl.multiple_of(b * block, block), block)
            for j in range(per):
                lanes = pl.ds(j * block, block)
                up_v[c, at, lanes] = up_v[c, at, lanes] * splat(keep_up[b, c * per + j], block)
                dn_v[c, lanes, at] = dn_v[c, lanes, at] * splat(keep_dn[c * per + j, b], block)

    def produce(s):
        t, c, k = lax.div(s, chunks), lax.rem(s, chunks), lax.rem(s, slots)

        @pl.when(t == 0)
        def _():
            for copy in weight_copies(c):
                copy.wait()
            apply_mask(c)

        token = pl.ds(pl.multiple_of(t * tm, tm), tm)
        h = jnp.dot(x[token, :], up_v[c], preferred_element_type=F32)
        g = lax.dot_general(ct[token, :], dn_v[c], NT, preferred_element_type=F32)

        @pl.when(s >= slots)
        def _():
            inward(k, True).wait_send()
            pl.semaphore_wait(cred_in, 1)

        @pl.when(has_outer)
        def _():
            outward_in(k).wait_recv()
            to_inner[k, 0] = (h + from_outer[k, 0].astype(F32)).astype(BF16)
            to_inner[k, 1] = (g + from_outer[k, 1].astype(F32)).astype(BF16)

            @pl.when(s + slots < steps)
            def _():
                pl.semaphore_signal(cred_in, inc=1, device_id=outer, device_id_type=MESH)

        @pl.when(jnp.logical_not(has_outer))
        def _():
            to_inner[k, 0] = h.astype(BF16)
            to_inner[k, 1] = g.astype(BF16)

        @pl.when(is_mid)
        def _():
            inward(k, True).start()

        @pl.when(jnp.logical_not(is_mid))
        def _():
            inward(k, False).start()

    def outward_in(k):
        return inward(k, False)

    def release(u):
        k = lax.rem(u, slots)
        for copy in stores(u):
            copy.wait()

        @pl.when(has_outer)
        def _():
            outward(k).wait_send()

        @pl.when(u + slots < steps)
        def _():
            @pl.when(is_mid)
            def _():
                pl.semaphore_signal(cred_in, inc=1, device_id=inner, device_id_type=MESH)

            @pl.when(jnp.logical_not(is_mid))
            def _():
                pl.semaphore_signal(cred_out, inc=1, device_id=inner, device_id_type=MESH)

    def consume(u):
        t, c, k = lax.div(u, chunks), lax.rem(u, chunks), lax.rem(u, slots)
        outward(k).wait_recv()

        @pl.when(is_mid)
        def _():
            h = to_inner[k, 0].astype(F32) + from_inner[k, 0].astype(F32)
            g = to_inner[k, 1].astype(F32) + from_inner[k, 1].astype(F32)
            active, slope = gelu_and_slope(h)
            from_inner[k, 0] = active.astype(BF16)
            from_inner[k, 1] = (g * slope).astype(BF16)

        @pl.when(has_outer)
        def _():
            @pl.when(u >= slots)
            def _():
                pl.semaphore_wait(cred_out, 1)

            outward(k).start()

        turned[k] = from_inner[k, 0].T
        for copy in stores(u):
            copy.start()
        acc[t, 0] += jnp.dot(from_inner[k, 0], dn_v[c], preferred_element_type=F32)
        acc[t, 1] += lax.dot_general(from_inner[k, 1], up_v[c], NT, preferred_element_type=F32)

        @pl.when(u >= DEFER)
        def _():
            release(u - DEFER)

    def rows_of(t, owner, first, count):
        return pl.ds(pl.multiple_of(t * tm + owner * (tm // 2) + first, part), count)

    def pair_copy(t):
        return pltpu.make_async_remote_copy(
            src_ref=pair_out.at[t], dst_ref=pair_in.at[t], send_sem=s0.at[t], recv_sem=r0.at[t],
            device_id=sibling, device_id_type=MESH)

    def chip_copy(t, j):
        return pltpu.make_async_remote_copy(
            src_ref=half.at[t, lax.rem(chip + j, chips)], dst_ref=chip_in.at[t, j - 1],
            send_sem=s1.at[t, j - 1], recv_sem=r1.at[t, j - 1],
            device_id=chip_peer(j), device_id_type=MESH)

    def spread_copy(t, j):
        mine = rows_of(t, core, chip * part, part)
        return pltpu.make_async_remote_copy(
            src_ref=fin.at[t], dst_ref=sums.at[:, mine, :],
            send_sem=s2.at[t, j - 1], recv_sem=r2.at[t, j - 1],
            device_id=chip_peer(j), device_id_type=MESH)

    def own_copy(t):
        mine = rows_of(t, core, chip * part, part)
        return pltpu.make_async_copy(fin.at[t], sums.at[:, mine, :], own_sem.at[t])

    def share_copy(t):
        mine = rows_of(t, core, 0, tm // 2)
        return pltpu.make_async_remote_copy(
            src_ref=sums.at[:, mine, :], dst_ref=sums.at[:, mine, :], send_sem=s3.at[t], recv_sem=r3.at[t],
            device_id=sibling, device_id_type=MESH)

    def phase0(t):
        other = pl.ds(pl.multiple_of((1 - core) * (tm // 2), tm // 2), tm // 2)
        for which in range(2):
            pair_out[t, which] = acc[t, which, other, :].astype(BF16)
        pair_copy(t).start()

    def phase1(t):
        pair_copy(t).wait()

        @pl.loop(0, chips)
        def _(q):
            mine = pl.ds(pl.multiple_of(core * (tm // 2) + q * part, part), part)
            there = pl.ds(pl.multiple_of(q * part, part), part)
            for which in range(2):
                half[t, q, which] = (acc[t, which, mine, :] + pair_in[t, which, there, :].astype(F32)).astype(BF16)

        for j in range(1, chips):
            chip_copy(t, j).start()

    def phase2(t):
        for j in range(1, chips):
            chip_copy(t, j).wait()
        for which in range(2):
            total = half[t, chip, which].astype(F32)
            for j in range(1, chips):
                total = total + chip_in[t, j - 1, which].astype(F32)
            fin[t, which] = total.astype(BF16)
        own_copy(t).start()
        for j in range(1, chips):
            spread_copy(t, j).start()

    def phase3(t):
        own_copy(t).wait()
        for j in range(1, chips):
            spread_copy(t, j).wait()
        share_copy(t).start()

    def phase4(t):
        share_copy(t).wait()

    phases = ((0, phase0), (2, phase1), (5, phase2), (8, phase3))
    late = []

    @pl.loop(0, steps + lag)
    def _(s):
        @pl.when(s < steps)
        def _():
            produce(s)

        @pl.when(s >= lag)
        def _():
            u = s - lag
            consume(u)
            for t in range(halves):
                for after, phase in phases:
                    at = (t + 1) * chunks - 1 + after
                    if at < steps:
                        @pl.when(u == at)
                        def _(phase=phase, t=t):
                            phase(t)

    for t in range(halves):
        for after, phase in phases:
            if (t + 1) * chunks - 1 + after >= steps:
                phase(t)
    for u in range(steps - DEFER, steps):
        release(u)

    @pl.loop(steps - slots, steps)
    def _(s):
        inward(lax.rem(s, slots), True).wait_send()

    for t in range(halves):
        phase4(t)


def grads_kernel(block, x, ct, act, hg, sums, keep_up, keep_dn, out, in_grad, up_out, dn_out, xt, sem):
    c = pl.program_id(0)
    width = hg.shape[1]
    per = width // block
    d_model = ct.shape[1]
    tall = 4 * block if d_model % (4 * block) == 0 else block
    moves = [pltpu.make_async_copy(sums.at[i], ref, sem.at[i]) for i, ref in enumerate((out, in_grad))]

    @pl.when(c == 0)
    def _():
        for move in moves:
            move.start()
        xt[...] = x[...].T

    for top in range(0, d_model, tall):
        full = jnp.dot(xt[top:top + tall, :], hg[...], preferred_element_type=F32)
        for i in range(0, tall, block):
            for j in range(per):
                lanes = slice(j * block, (j + 1) * block)
                keep = keep_up[(top + i) // block, c * per + j].astype(F32)
                up_out[top + i:top + i + block, lanes] = (full[i:i + block, lanes] * keep).astype(BF16)
        there = slice(top, top + tall)
        full = jnp.dot(act[...], ct[:, there], preferred_element_type=F32)
        for j in range(per):
            lanes = slice(j * block, (j + 1) * block)
            for i in range(0, tall, block):
                keep = keep_dn[c * per + j, (top + i) // block].astype(F32)
                dn_out[lanes, top + i:top + i + block] = (full[lanes, i:i + block] * keep).astype(BF16)

    @pl.when(c == pl.num_programs(0) - 1)
    def _():
        for move in moves:
            move.wait()


def body(rows, cols, inputs, up_weight, down_weight, up_mask, down_mask, cotangent):
    tokens, d_model = inputs.shape
    hidden = up_weight.shape[1]
    block = d_model // up_mask.shape[0]
    width = 2 * block if hidden % (2 * block) == 0 else block
    chunks = hidden // width
    halves = next(h for h in (4, 2, 1) if tokens % (h * cols * 16) == 0)
    tm = tokens // halves
    chips = cols // 2
    part = tm // cols
    slots = min(3 * halves, halves * chunks)
    vmem = pl.BlockSpec(memory_space=pltpu.VMEM)
    smem = pl.BlockSpec(memory_space=pltpu.SMEM)
    hbm = pl.BlockSpec(memory_space=pl.ANY)
    dma = pltpu.SemaphoreType.DMA
    sums, act, hg = pl.pallas_call(
        functools.partial(layer_kernel, rows, cols, halves, width, block, slots),
        out_shape=(
            jax.ShapeDtypeStruct((2, tokens, d_model), BF16),
            jax.ShapeDtypeStruct((hidden, tokens), BF16),
            jax.ShapeDtypeStruct((tokens, hidden), BF16),
        ),
        in_specs=[vmem, vmem, hbm, hbm, smem, smem],
        out_specs=(hbm, hbm, hbm),
        scratch_shapes=[
            pltpu.VMEM((chunks, d_model, width), BF16),
            pltpu.VMEM((chunks, width, d_model), BF16),
            pltpu.VMEM((halves, 2, tm, d_model), F32),
            pltpu.VMEM((slots, 2, tm, width), BF16),
            pltpu.VMEM((slots, 2, tm, width), BF16),
            pltpu.VMEM((slots, 2, tm, width), BF16),
            pltpu.VMEM((slots, width, tm), BF16),
            pltpu.VMEM((halves, 2, tm // 2, d_model), BF16),
            pltpu.VMEM((halves, 2, tm // 2, d_model), BF16),
            pltpu.VMEM((halves, chips, 2, part, d_model), BF16),
            pltpu.VMEM((halves, max(chips - 1, 1), 2, part, d_model), BF16),
            pltpu.VMEM((halves, 2, part, d_model), BF16),
            dma((2, chunks)),
            dma((slots,)), dma((slots,)), dma((slots,)), dma((slots,)),
            dma((2, slots)),
            pltpu.SemaphoreType.REGULAR, pltpu.SemaphoreType.REGULAR,
            dma((halves,)), dma((halves,)),
            dma((halves, max(chips - 1, 1))), dma((halves, max(chips - 1, 1))),
            dma((halves, max(chips - 1, 1))), dma((halves, max(chips - 1, 1))),
            dma((halves,)), dma((halves,)),
            dma((halves,)),
        ],
        compiler_params=pltpu.CompilerParams(collective_id=0, has_side_effects=True, vmem_limit_bytes=LIMIT),
        cost_estimate=pl.CostEstimate(
            flops=8 * tokens * d_model * hidden, bytes_accessed=4 * d_model * hidden, transcendentals=tokens * hidden),
    )(inputs, cotangent, up_weight, down_weight, up_mask, down_mask)

    wide = next(w for w in (4 * block, 2 * block, block) if hidden % w == 0)
    output, input_grad, up_grad, down_grad = pl.pallas_call(
        functools.partial(grads_kernel, block),
        grid=(hidden // wide,),
        out_shape=(
            jax.ShapeDtypeStruct((tokens, d_model), BF16),
            jax.ShapeDtypeStruct((tokens, d_model), BF16),
            jax.ShapeDtypeStruct((d_model, hidden), BF16),
            jax.ShapeDtypeStruct((hidden, d_model), BF16),
        ),
        in_specs=[
            pl.BlockSpec((tokens, d_model), lambda c: (0, 0)),
            pl.BlockSpec((tokens, d_model), lambda c: (0, 0)),
            pl.BlockSpec((wide, tokens), lambda c: (c, 0)),
            pl.BlockSpec((tokens, wide), lambda c: (0, c)),
            hbm, smem, smem,
        ],
        out_specs=(
            hbm, hbm,
            pl.BlockSpec((d_model, wide), lambda c: (0, c)),
            pl.BlockSpec((wide, d_model), lambda c: (c, 0)),
        ),
        scratch_shapes=[pltpu.VMEM((d_model, tokens), BF16), dma((2,))],
        compiler_params=pltpu.CompilerParams(vmem_limit_bytes=48 * 1024 * 1024),
        cost_estimate=pl.CostEstimate(
            flops=4 * tokens * d_model * hidden, bytes_accessed=4 * d_model * hidden, transcendentals=0),
    )(inputs, cotangent, act, hg, sums, up_mask, down_mask)
    return (output, input_grad, up_grad, down_grad)


def solution(mesh):
    in_specs = (
        P(None, "row"),
        P("row", "col"),
        P("col", "row"),
        P("row", "col"),
        P("col", "row"),
        P(None, "row"),
    )
    out_specs = (P(None, "row"), P(None, "row"), P("row", "col"), P("col", "row"))
    step = functools.partial(body, mesh.shape["row"], mesh.shape["col"])
    return jax.shard_map(step, mesh=mesh, in_specs=in_specs, out_specs=out_specs, check_vma=False)
```

```python
import functools

import jax
import jax.numpy as jnp
from jax import lax
from jax.experimental import pallas as pl
from jax.experimental.pallas import tpu as pltpu
from jax.sharding import PartitionSpec as P

MESH = pl.DeviceIdType.MESH
F32 = jnp.float32
BF16 = jnp.bfloat16
DEFER = 2
LIMIT = 63 * 1024 * 1024
NT = (((1,), (1,)), ((), ()))
TN = (((0,), (0,)), ((), ()))
ROOT = 0.7978845608028654
CUBE = 0.044715


def gelu_and_slope(v):
    square = v * v
    tanh = jnp.tanh(ROOT * v * (1.0 + CUBE * square))
    half = 0.5 * (1.0 + tanh)
    slope = half + 0.5 * v * (1.0 - tanh * tanh) * (ROOT * (1.0 + 3.0 * CUBE * square))
    return v * half, slope


def splat(keep, block):
    tile = jnp.full((16, block), keep.astype(F32)).astype(BF16)
    return jnp.broadcast_to(tile[None], (block // 16, 16, block)).reshape(block, block)


def layer_kernel(
    rows, cols, halves, width, block, slots,
    x, ct, up_hbm, dn_hbm, keep_up, keep_dn,
    sums, act_hbm, hg_hbm,
    up_v, dn_v, acc, to_inner, from_outer, from_inner, turned,
    pair_out, pair_in, half, chip_in, share_in,
    w_sem, in_send, out_recv, in_recv, out_send, store_sem, cred_in, cred_out,
    s0, r0, s1, r1, s2, r2, s3, r3, own_sem,
):
    tokens, d_model = x.shape
    chunks = up_v.shape[0]
    tm = tokens // halves
    steps = halves * chunks
    chips = cols // 2
    part = tm // cols
    me_r, me_c = lax.axis_index("row"), lax.axis_index("col")
    chip, core = lax.div(me_c, 2), lax.rem(me_c, 2)
    sibling = (me_r, chip * 2 + 1 - core)
    mid = rows // 2
    left = me_r < mid
    toward = jnp.where(left, 1, -1)
    dist = jnp.where(left, mid - 1 - me_r, me_r - mid)
    is_mid = dist == 0
    has_outer = jnp.logical_and(me_r > 0, me_r < rows - 1)
    inner = (me_r + toward, me_c)
    outer = (lax.rem(me_r - toward + rows, rows), me_c)
    lag = 2 + 3 * dist

    def chip_peer(j):
        return (me_r, lax.rem(chip + j, chips) * 2 + core)

    def weight_copies(c):
        at = pl.multiple_of(c * width, width)
        return (
            pltpu.make_async_copy(up_hbm.at[:, pl.ds(at, width)], up_v.at[c], w_sem.at[0, c]),
            pltpu.make_async_copy(dn_hbm.at[pl.ds(at, width), :], dn_v.at[c], w_sem.at[1, c]),
        )

    @pl.loop(0, chunks)
    def _(c):
        for copy in weight_copies(c):
            copy.start()

    barrier = pltpu.get_barrier_semaphore()
    greet = [inner, sibling] + [chip_peer(j) for j in range(1, chips)]
    for device in greet:
        pl.semaphore_signal(barrier, inc=1, device_id=device, device_id_type=MESH)

    @pl.when(has_outer)
    def _():
        pl.semaphore_signal(barrier, inc=1, device_id=outer, device_id_type=MESH)

    for t in range(halves):
        for which in range(2):
            acc[t, which] = jnp.zeros((tm, d_model), F32)

    @pl.when(has_outer)
    def _():
        pl.semaphore_wait(barrier, len(greet) + 1)

    @pl.when(jnp.logical_not(has_outer))
    def _():
        pl.semaphore_wait(barrier, len(greet))

    def inward(k, middle):
        return pltpu.make_async_remote_copy(
            src_ref=to_inner.at[k],
            dst_ref=from_inner.at[k] if middle else from_outer.at[k],
            send_sem=in_send.at[k],
            recv_sem=in_recv.at[k] if middle else out_recv.at[k],
            device_id=inner,
            device_id_type=MESH,
        )

    def outward(k):
        return pltpu.make_async_remote_copy(
            src_ref=from_inner.at[k],
            dst_ref=from_inner.at[k],
            send_sem=out_send.at[k],
            recv_sem=in_recv.at[k],
            device_id=outer,
            device_id_type=MESH,
        )

    def stores(u):
        k = lax.rem(u, slots)
        row = pl.multiple_of(lax.div(u, chunks) * tm, tm)
        col = pl.multiple_of(lax.rem(u, chunks) * width, width)
        token, unit = pl.ds(row, tm), pl.ds(col, width)
        return (
            pltpu.make_async_copy(turned.at[k], act_hbm.at[unit, token], store_sem.at[0, k]),
            pltpu.make_async_copy(from_inner.at[k, 1], hg_hbm.at[token, unit], store_sem.at[1, k]),
        )

    def apply_mask(c):
        per = width // block

        @pl.loop(0, d_model // block)
        def _(b):
            at = pl.ds(pl.multiple_of(b * block, block), block)
            for j in range(per):
                lanes = pl.ds(j * block, block)
                up_v[c, at, lanes] = up_v[c, at, lanes] * splat(keep_up[b, c * per + j], block)
                dn_v[c, lanes, at] = dn_v[c, lanes, at] * splat(keep_dn[c * per + j, b], block)

    def produce(s):
        t, c, k = lax.div(s, chunks), lax.rem(s, chunks), lax.rem(s, slots)

        @pl.when(t == 0)
        def _():
            for copy in weight_copies(c):
                copy.wait()
            apply_mask(c)

        token = pl.ds(pl.multiple_of(t * tm, tm), tm)
        h = jnp.dot(x[token, :], up_v[c], preferred_element_type=F32)
        g = lax.dot_general(ct[token, :], dn_v[c], NT, preferred_element_type=F32)

        @pl.when(s >= slots)
        def _():
            inward(k, True).wait_send()
            pl.semaphore_wait(cred_in, 1)

        @pl.when(has_outer)
        def _():
            outward_in(k).wait_recv()
            to_inner[k, 0] = (h + from_outer[k, 0].astype(F32)).astype(BF16)
            to_inner[k, 1] = (g + from_outer[k, 1].astype(F32)).astype(BF16)

            @pl.when(s + slots < steps)
            def _():
                pl.semaphore_signal(cred_in, inc=1, device_id=outer, device_id_type=MESH)

        @pl.when(jnp.logical_not(has_outer))
        def _():
            to_inner[k, 0] = h.astype(BF16)
            to_inner[k, 1] = g.astype(BF16)

        @pl.when(is_mid)
        def _():
            inward(k, True).start()

        @pl.when(jnp.logical_not(is_mid))
        def _():
            inward(k, False).start()

    def outward_in(k):
        return inward(k, False)

    def release(u):
        k = lax.rem(u, slots)
        for copy in stores(u):
            copy.wait()

        @pl.when(has_outer)
        def _():
            outward(k).wait_send()

        @pl.when(u + slots < steps)
        def _():
            @pl.when(is_mid)
            def _():
                pl.semaphore_signal(cred_in, inc=1, device_id=inner, device_id_type=MESH)

            @pl.when(jnp.logical_not(is_mid))
            def _():
                pl.semaphore_signal(cred_out, inc=1, device_id=inner, device_id_type=MESH)

    def consume(u):
        t, c, k = lax.div(u, chunks), lax.rem(u, chunks), lax.rem(u, slots)
        outward(k).wait_recv()

        @pl.when(is_mid)
        def _():
            h = to_inner[k, 0].astype(F32) + from_inner[k, 0].astype(F32)
            g = to_inner[k, 1].astype(F32) + from_inner[k, 1].astype(F32)
            active, slope = gelu_and_slope(h)
            from_inner[k, 0] = active.astype(BF16)
            from_inner[k, 1] = (g * slope).astype(BF16)

        @pl.when(has_outer)
        def _():
            @pl.when(u >= slots)
            def _():
                pl.semaphore_wait(cred_out, 1)

            outward(k).start()

        turned[k] = from_inner[k, 0].T
        for copy in stores(u):
            copy.start()
        acc[t, 0] += jnp.dot(from_inner[k, 0], dn_v[c], preferred_element_type=F32)
        acc[t, 1] += lax.dot_general(from_inner[k, 1], up_v[c], NT, preferred_element_type=F32)

        @pl.when(u >= DEFER)
        def _():
            release(u - DEFER)

    def rows_of(t, owner, first, count):
        return pl.ds(pl.multiple_of(t * tm + owner * (tm // 2) + first, part), count)

    def pair_copy(t):
        return pltpu.make_async_remote_copy(
            src_ref=pair_out.at[t], dst_ref=pair_in.at[t], send_sem=s0.at[t], recv_sem=r0.at[t],
            device_id=sibling, device_id_type=MESH)

    def chip_copy(t, j):
        return pltpu.make_async_remote_copy(
            src_ref=half.at[t, lax.rem(chip + j, chips)], dst_ref=chip_in.at[t, j - 1],
            send_sem=s1.at[t, j - 1], recv_sem=r1.at[t, j - 1],
            device_id=chip_peer(j), device_id_type=MESH)

    mine = pl.ds(pl.multiple_of(chip * part, part), part)

    def spread_copy(t, j):
        place = pair_out.at[t, :, mine, :]
        return pltpu.make_async_remote_copy(
            src_ref=place, dst_ref=place, send_sem=s2.at[t, j - 1], recv_sem=r2.at[t, j - 1],
            device_id=chip_peer(j), device_id_type=MESH)

    def share_copy(t):
        return pltpu.make_async_remote_copy(
            src_ref=pair_out.at[t], dst_ref=share_in.at[t], send_sem=s3.at[t], recv_sem=r3.at[t],
            device_id=sibling, device_id_type=MESH)

    def own_store(t):
        return pltpu.make_async_copy(pair_out.at[t], sums.at[:, rows_of(t, core, 0, tm // 2), :], own_sem.at[t, 0])

    def share_store(t):
        return pltpu.make_async_copy(share_in.at[t], sums.at[:, rows_of(t, 1 - core, 0, tm // 2), :], own_sem.at[t, 1])

    def phase0(t):
        other = pl.ds(pl.multiple_of((1 - core) * (tm // 2), tm // 2), tm // 2)
        for which in range(2):
            pair_out[t, which] = acc[t, which, other, :].astype(BF16)
        pair_copy(t).start()

    def phase1(t):
        pair_copy(t).wait()

        @pl.loop(0, chips)
        def _(q):
            held = pl.ds(pl.multiple_of(core * (tm // 2) + q * part, part), part)
            there = pl.ds(pl.multiple_of(q * part, part), part)
            for which in range(2):
                half[t, q, which] = (acc[t, which, held, :] + pair_in[t, which, there, :].astype(F32)).astype(BF16)

        for j in range(1, chips):
            chip_copy(t, j).start()

    def phase2(t):
        for j in range(1, chips):
            chip_copy(t, j).wait()
        for which in range(2):
            total = half[t, chip, which].astype(F32)
            for j in range(1, chips):
                total = total + chip_in[t, j - 1, which].astype(F32)
            pair_out[t, which, mine, :] = total.astype(BF16)
        for j in range(1, chips):
            spread_copy(t, j).start()

    def phase3(t):
        for j in range(1, chips):
            spread_copy(t, j).wait()
        share_copy(t).start()
        own_store(t).start()

    def phase4(t):
        share_copy(t).wait()
        share_store(t).start()
        own_store(t).wait()
        share_store(t).wait()

    phases = ((0, phase0), (2, phase1), (5, phase2), (8, phase3))
    late = []

    @pl.loop(0, steps + lag)
    def _(s):
        @pl.when(s < steps)
        def _():
            produce(s)

        @pl.when(s >= lag)
        def _():
            u = s - lag
            consume(u)
            for t in range(halves):
                for after, phase in phases:
                    at = (t + 1) * chunks - 1 + after
                    if at < steps:
                        @pl.when(u == at)
                        def _(phase=phase, t=t):
                            phase(t)

    for t in range(halves):
        for after, phase in phases:
            if (t + 1) * chunks - 1 + after >= steps:
                phase(t)
    for u in range(steps - DEFER, steps):
        release(u)

    @pl.loop(steps - slots, steps)
    def _(s):
        inward(lax.rem(s, slots), True).wait_send()

    for t in range(halves):
        phase4(t)


def grads_kernel(block, x, ct, act, hg, sums, keep_up, keep_dn, out, in_grad, up_out, dn_out, xt):
    c = pl.program_id(0)
    width = hg.shape[1]
    per = width // block
    d_model = ct.shape[1]
    tall = next(b for b in (4 * block, 2 * block, block) if d_model % b == 0)
    out[...] = sums[0]
    in_grad[...] = sums[1]

    @pl.when(c == 0)
    def _():
        xt[...] = x[...].T

    @pl.loop(0, d_model // tall)
    def _(b):
        top = pl.multiple_of(b * tall, tall)
        there = pl.ds(top, tall)
        up = jnp.dot(xt[there, :], hg[...], preferred_element_type=F32)
        dn = jnp.dot(act[...], ct[:, there], preferred_element_type=F32)
        for i in range(0, tall, block):
            place = pl.ds(pl.multiple_of(top + i, block), block)
            which = b * (tall // block) + i // block
            for j in range(per):
                lanes = slice(j * block, (j + 1) * block)
                keep = keep_up[which, c * per + j].astype(F32)
                up_out[place, lanes] = (up[i:i + block, lanes] * keep).astype(BF16)
                keep = keep_dn[c * per + j, which].astype(F32)
                dn_out[lanes, place] = (dn[lanes, i:i + block] * keep).astype(BF16)


def body(rows, cols, inputs, up_weight, down_weight, up_mask, down_mask, cotangent):
    tokens, d_model = inputs.shape
    hidden = up_weight.shape[1]
    block = d_model // up_mask.shape[0]
    width = 2 * block if hidden % (2 * block) == 0 else block
    chunks = hidden // width
    halves = next(h for h in (4, 2, 1) if tokens % (h * cols * 16) == 0)
    tm = tokens // halves
    chips = cols // 2
    part = tm // cols
    slots = min(3 * halves, halves * chunks)
    vmem = pl.BlockSpec(memory_space=pltpu.VMEM)
    smem = pl.BlockSpec(memory_space=pltpu.SMEM)
    hbm = pl.BlockSpec(memory_space=pl.ANY)
    dma = pltpu.SemaphoreType.DMA
    sums, act, hg = pl.pallas_call(
        functools.partial(layer_kernel, rows, cols, halves, width, block, slots),
        out_shape=(
            jax.ShapeDtypeStruct((2, tokens, d_model), BF16),
            jax.ShapeDtypeStruct((hidden, tokens), BF16),
            jax.ShapeDtypeStruct((tokens, hidden), BF16),
        ),
        in_specs=[vmem, vmem, hbm, hbm, smem, smem],
        out_specs=(hbm, hbm, hbm),
        scratch_shapes=[
            pltpu.VMEM((chunks, d_model, width), BF16),
            pltpu.VMEM((chunks, width, d_model), BF16),
            pltpu.VMEM((halves, 2, tm, d_model), F32),
            pltpu.VMEM((slots, 2, tm, width), BF16),
            pltpu.VMEM((slots, 2, tm, width), BF16),
            pltpu.VMEM((slots, 2, tm, width), BF16),
            pltpu.VMEM((slots, width, tm), BF16),
            pltpu.VMEM((halves, 2, tm // 2, d_model), BF16),
            pltpu.VMEM((halves, 2, tm // 2, d_model), BF16),
            pltpu.VMEM((halves, chips, 2, part, d_model), BF16),
            pltpu.VMEM((halves, max(chips - 1, 1), 2, part, d_model), BF16),
            pltpu.VMEM((halves, 2, tm // 2, d_model), BF16),
            dma((2, chunks)),
            dma((slots,)), dma((slots,)), dma((slots,)), dma((slots,)),
            dma((2, slots)),
            pltpu.SemaphoreType.REGULAR, pltpu.SemaphoreType.REGULAR,
            dma((halves,)), dma((halves,)),
            dma((halves, max(chips - 1, 1))), dma((halves, max(chips - 1, 1))),
            dma((halves, max(chips - 1, 1))), dma((halves, max(chips - 1, 1))),
            dma((halves,)), dma((halves,)),
            dma((halves, 2)),
        ],
        compiler_params=pltpu.CompilerParams(collective_id=0, has_side_effects=True, vmem_limit_bytes=LIMIT),
        cost_estimate=pl.CostEstimate(
            flops=8 * tokens * d_model * hidden, bytes_accessed=4 * d_model * hidden, transcendentals=tokens * hidden),
    )(inputs, cotangent, up_weight, down_weight, up_mask, down_mask)

    wide = next(w for w in (4 * block, 2 * block, block) if hidden % w == 0)
    pieces = next(n for n in (4, 2, 1) if n <= hidden // wide and tokens % (n * 16) == 0)
    output, input_grad, up_grad, down_grad = pl.pallas_call(
        functools.partial(grads_kernel, block),
        grid=(hidden // wide,),
        out_shape=(
            jax.ShapeDtypeStruct((tokens, d_model), BF16),
            jax.ShapeDtypeStruct((tokens, d_model), BF16),
            jax.ShapeDtypeStruct((d_model, hidden), BF16),
            jax.ShapeDtypeStruct((hidden, d_model), BF16),
        ),
        in_specs=[
            pl.BlockSpec((tokens, d_model), lambda c: (0, 0)),
            pl.BlockSpec((tokens, d_model), lambda c: (0, 0)),
            pl.BlockSpec((wide, tokens), lambda c: (c, 0)),
            pl.BlockSpec((tokens, wide), lambda c: (0, c)),
            pl.BlockSpec((2, tokens // pieces, d_model), lambda c: (0, jnp.minimum(c, pieces - 1), 0)),
            smem, smem,
        ],
        out_specs=(
            pl.BlockSpec((tokens // pieces, d_model), lambda c: (jnp.minimum(c, pieces - 1), 0)),
            pl.BlockSpec((tokens // pieces, d_model), lambda c: (jnp.minimum(c, pieces - 1), 0)),
            pl.BlockSpec((d_model, wide), lambda c: (0, c)),
            pl.BlockSpec((wide, d_model), lambda c: (c, 0)),
        ),
        scratch_shapes=[pltpu.VMEM((d_model, tokens), BF16)],
        compiler_params=pltpu.CompilerParams(vmem_limit_bytes=LIMIT),
        cost_estimate=pl.CostEstimate(
            flops=4 * tokens * d_model * hidden, bytes_accessed=4 * d_model * hidden, transcendentals=0),
    )(inputs, cotangent, act, hg, sums, up_mask, down_mask)
    return (output, input_grad, up_grad, down_grad)


def solution(mesh):
    in_specs = (
        P(None, "row"),
        P("row", "col"),
        P("col", "row"),
        P("row", "col"),
        P("col", "row"),
        P(None, "row"),
    )
    out_specs = (P(None, "row"), P(None, "row"), P("row", "col"), P("col", "row"))
    step = functools.partial(body, mesh.shape["row"], mesh.shape["col"])
    return jax.shard_map(step, mesh=mesh, in_specs=in_specs, out_specs=out_specs, check_vma=False)
```

```python
import functools

import jax
import jax.numpy as jnp
from jax import lax
from jax.experimental import pallas as pl
from jax.experimental.pallas import tpu as pltpu
from jax.sharding import PartitionSpec as P

MESH = pl.DeviceIdType.MESH
F32 = jnp.float32
BF16 = jnp.bfloat16
DEFER = 2
LIMIT = 63 * 1024 * 1024
NT = (((1,), (1,)), ((), ()))
TN = (((0,), (0,)), ((), ()))
ROOT = 0.7978845608028654
CUBE = 0.044715


def gelu_and_slope(v):
    square = v * v
    tanh = jnp.tanh(ROOT * v * (1.0 + CUBE * square))
    half = 0.5 * (1.0 + tanh)
    slope = half + 0.5 * v * (1.0 - tanh * tanh) * (ROOT * (1.0 + 3.0 * CUBE * square))
    return v * half, slope


def splat(keep, block):
    tile = jnp.full((16, block), keep.astype(F32)).astype(BF16)
    return jnp.broadcast_to(tile[None], (block // 16, 16, block)).reshape(block, block)


def layer_kernel(
    rows, cols, halves, width, block, slots,
    x, ct, up_hbm, dn_hbm, keep_up, keep_dn,
    sums, act_hbm, hg_hbm,
    up_v, dn_v, acc, to_inner, from_outer, from_inner, turned,
    pair_out, pair_in, half, chip_in, share_in,
    w_sem, in_send, out_recv, in_recv, out_send, store_sem, cred_in, cred_out,
    s0, r0, s1, r1, s2, r2, s3, r3, own_sem,
):
    tokens, d_model = x.shape
    chunks = up_v.shape[0]
    tm = tokens // halves
    steps = halves * chunks
    chips = cols // 2
    part = tm // cols
    me_r, me_c = lax.axis_index("row"), lax.axis_index("col")
    chip, core = lax.div(me_c, 2), lax.rem(me_c, 2)
    sibling = (me_r, chip * 2 + 1 - core)
    mid = rows // 2
    left = me_r < mid
    toward = jnp.where(left, 1, -1)
    dist = jnp.where(left, mid - 1 - me_r, me_r - mid)
    is_mid = dist == 0
    has_outer = jnp.logical_and(me_r > 0, me_r < rows - 1)
    inner = (me_r + toward, me_c)
    outer = (lax.rem(me_r - toward + rows, rows), me_c)
    lag = 2 + 3 * dist

    def chip_peer(j):
        return (me_r, lax.rem(chip + j, chips) * 2 + core)

    def weight_copies(c):
        at = pl.multiple_of(c * width, width)
        return (
            pltpu.make_async_copy(up_hbm.at[:, pl.ds(at, width)], up_v.at[c], w_sem.at[0, c]),
            pltpu.make_async_copy(dn_hbm.at[pl.ds(at, width), :], dn_v.at[c], w_sem.at[1, c]),
        )

    @pl.loop(0, chunks)
    def _(c):
        for copy in weight_copies(c):
            copy.start()

    barrier = pltpu.get_barrier_semaphore()
    greet = [inner, sibling] + [chip_peer(j) for j in range(1, chips)]
    for device in greet:
        pl.semaphore_signal(barrier, inc=1, device_id=device, device_id_type=MESH)

    @pl.when(has_outer)
    def _():
        pl.semaphore_signal(barrier, inc=1, device_id=outer, device_id_type=MESH)

    for t in range(halves):
        for which in range(2):
            acc[t, which] = jnp.zeros((tm, d_model), F32)

    @pl.when(has_outer)
    def _():
        pl.semaphore_wait(barrier, len(greet) + 1)

    @pl.when(jnp.logical_not(has_outer))
    def _():
        pl.semaphore_wait(barrier, len(greet))

    def inward(k, middle):
        return pltpu.make_async_remote_copy(
            src_ref=to_inner.at[k],
            dst_ref=from_inner.at[k] if middle else from_outer.at[k],
            send_sem=in_send.at[k],
            recv_sem=in_recv.at[k] if middle else out_recv.at[k],
            device_id=inner,
            device_id_type=MESH,
        )

    def outward(k):
        return pltpu.make_async_remote_copy(
            src_ref=from_inner.at[k],
            dst_ref=from_inner.at[k],
            send_sem=out_send.at[k],
            recv_sem=in_recv.at[k],
            device_id=outer,
            device_id_type=MESH,
        )

    def stores(u):
        k = lax.rem(u, slots)
        row = pl.multiple_of(lax.div(u, chunks) * tm, tm)
        col = pl.multiple_of(lax.rem(u, chunks) * width, width)
        token, unit = pl.ds(row, tm), pl.ds(col, width)
        return (
            pltpu.make_async_copy(turned.at[k], act_hbm.at[unit, token], store_sem.at[0, k]),
            pltpu.make_async_copy(from_inner.at[k, 1], hg_hbm.at[token, unit], store_sem.at[1, k]),
        )

    def apply_mask(c):
        per = width // block

        @pl.loop(0, d_model // block)
        def _(b):
            at = pl.ds(pl.multiple_of(b * block, block), block)
            for j in range(per):
                lanes = pl.ds(j * block, block)
                up_v[c, at, lanes] = up_v[c, at, lanes] * splat(keep_up[b, c * per + j], block)
                dn_v[c, lanes, at] = dn_v[c, lanes, at] * splat(keep_dn[c * per + j, b], block)

    def produce(s):
        t, c, k = lax.div(s, chunks), lax.rem(s, chunks), lax.rem(s, slots)

        @pl.when(t == 0)
        def _():
            for copy in weight_copies(c):
                copy.wait()
            apply_mask(c)

        token = pl.ds(pl.multiple_of(t * tm, tm), tm)
        h = jnp.dot(x[token, :], up_v[c], preferred_element_type=F32)
        g = lax.dot_general(ct[token, :], dn_v[c], NT, preferred_element_type=F32)

        @pl.when(s >= slots)
        def _():
            inward(k, True).wait_send()
            pl.semaphore_wait(cred_in, 1)

        @pl.when(has_outer)
        def _():
            outward_in(k).wait_recv()
            to_inner[k, 0] = (h + from_outer[k, 0].astype(F32)).astype(BF16)
            to_inner[k, 1] = (g + from_outer[k, 1].astype(F32)).astype(BF16)

            @pl.when(s + slots < steps)
            def _():
                pl.semaphore_signal(cred_in, inc=1, device_id=outer, device_id_type=MESH)

        @pl.when(jnp.logical_not(has_outer))
        def _():
            to_inner[k, 0] = h.astype(BF16)
            to_inner[k, 1] = g.astype(BF16)

        @pl.when(is_mid)
        def _():
            inward(k, True).start()

        @pl.when(jnp.logical_not(is_mid))
        def _():
            inward(k, False).start()

    def outward_in(k):
        return inward(k, False)

    def release(u):
        k = lax.rem(u, slots)
        for copy in stores(u):
            copy.wait()

        @pl.when(has_outer)
        def _():
            outward(k).wait_send()

        @pl.when(u + slots < steps)
        def _():
            @pl.when(is_mid)
            def _():
                pl.semaphore_signal(cred_in, inc=1, device_id=inner, device_id_type=MESH)

            @pl.when(jnp.logical_not(is_mid))
            def _():
                pl.semaphore_signal(cred_out, inc=1, device_id=inner, device_id_type=MESH)

    def consume(u):
        t, c, k = lax.div(u, chunks), lax.rem(u, chunks), lax.rem(u, slots)
        outward(k).wait_recv()

        @pl.when(is_mid)
        def _():
            h = to_inner[k, 0].astype(F32) + from_inner[k, 0].astype(F32)
            g = to_inner[k, 1].astype(F32) + from_inner[k, 1].astype(F32)
            active, slope = gelu_and_slope(h)
            from_inner[k, 0] = active.astype(BF16)
            from_inner[k, 1] = (g * slope).astype(BF16)

        @pl.when(has_outer)
        def _():
            @pl.when(u >= slots)
            def _():
                pl.semaphore_wait(cred_out, 1)

            outward(k).start()

        turned[k] = from_inner[k, 0].T
        for copy in stores(u):
            copy.start()
        acc[t, 0] += jnp.dot(from_inner[k, 0], dn_v[c], preferred_element_type=F32)
        acc[t, 1] += lax.dot_general(from_inner[k, 1], up_v[c], NT, preferred_element_type=F32)

        @pl.when(u >= DEFER)
        def _():
            release(u - DEFER)

    def rows_of(t, owner, first, count):
        return pl.ds(pl.multiple_of(t * tm + owner * (tm // 2) + first, part), count)

    def pair_copy(t):
        return pltpu.make_async_remote_copy(
            src_ref=pair_out.at[t], dst_ref=pair_in.at[t], send_sem=s0.at[t], recv_sem=r0.at[t],
            device_id=sibling, device_id_type=MESH)

    def chip_copy(t, j):
        return pltpu.make_async_remote_copy(
            src_ref=half.at[t, lax.rem(chip + j, chips)], dst_ref=chip_in.at[t, j - 1],
            send_sem=s1.at[t, j - 1], recv_sem=r1.at[t, j - 1],
            device_id=chip_peer(j), device_id_type=MESH)

    mine = pl.ds(pl.multiple_of(chip * part, part), part)

    def spread_copy(t, j):
        place = pair_out.at[t, :, mine, :]
        return pltpu.make_async_remote_copy(
            src_ref=place, dst_ref=place, send_sem=s2.at[t, j - 1], recv_sem=r2.at[t, j - 1],
            device_id=chip_peer(j), device_id_type=MESH)

    def share_copy(t):
        return pltpu.make_async_remote_copy(
            src_ref=pair_out.at[t], dst_ref=share_in.at[t], send_sem=s3.at[t], recv_sem=r3.at[t],
            device_id=sibling, device_id_type=MESH)

    def own_store(t):
        return pltpu.make_async_copy(pair_out.at[t], sums.at[:, rows_of(t, core, 0, tm // 2), :], own_sem.at[t, 0])

    def share_store(t):
        return pltpu.make_async_copy(share_in.at[t], sums.at[:, rows_of(t, 1 - core, 0, tm // 2), :], own_sem.at[t, 1])

    def phase0(t):
        other = pl.ds(pl.multiple_of((1 - core) * (tm // 2), tm // 2), tm // 2)
        for which in range(2):
            pair_out[t, which] = acc[t, which, other, :].astype(BF16)
        pair_copy(t).start()

    def phase1(t):
        pair_copy(t).wait()

        @pl.loop(0, chips)
        def _(q):
            held = pl.ds(pl.multiple_of(core * (tm // 2) + q * part, part), part)
            there = pl.ds(pl.multiple_of(q * part, part), part)
            for which in range(2):
                half[t, q, which] = (acc[t, which, held, :] + pair_in[t, which, there, :].astype(F32)).astype(BF16)

        for j in range(1, chips):
            chip_copy(t, j).start()

    def phase2(t):
        for j in range(1, chips):
            chip_copy(t, j).wait()
        for which in range(2):
            total = half[t, chip, which].astype(F32)
            for j in range(1, chips):
                total = total + chip_in[t, j - 1, which].astype(F32)
            pair_out[t, which, mine, :] = total.astype(BF16)
        for j in range(1, chips):
            spread_copy(t, j).start()

    def phase3(t):
        for j in range(1, chips):
            spread_copy(t, j).wait()
        share_copy(t).start()
        own_store(t).start()

    def phase4(t):
        share_copy(t).wait()
        share_store(t).start()
        own_store(t).wait()
        share_store(t).wait()

    phases = ((0, phase0), (2, phase1), (5, phase2), (8, phase3))
    late = []

    @pl.loop(0, steps + lag)
    def _(s):
        @pl.when(s < steps)
        def _():
            produce(s)

        @pl.when(s >= lag)
        def _():
            u = s - lag
            consume(u)
            for t in range(halves):
                for after, phase in phases:
                    at = (t + 1) * chunks - 1 + after
                    if at < steps:
                        @pl.when(u == at)
                        def _(phase=phase, t=t):
                            phase(t)

    for t in range(halves):
        for after, phase in phases:
            if (t + 1) * chunks - 1 + after >= steps:
                phase(t)
    for u in range(steps - DEFER, steps):
        release(u)

    @pl.loop(steps - slots, steps)
    def _(s):
        inward(lax.rem(s, slots), True).wait_send()

    for t in range(halves):
        phase4(t)


def grads_kernel(block, x, ct, act, hg, sums, keep_up, keep_dn, out, in_grad, up_out, dn_out, xt):
    c = pl.program_id(0)
    width = hg.shape[1]
    per = width // block
    d_model = ct.shape[1]
    tall = next(b for b in (4 * block, 2 * block, block) if d_model % b == 0)
    out[...] = sums[0]
    in_grad[...] = sums[1]

    @pl.when(c == 0)
    def _():
        xt[...] = x[...].T

    @pl.loop(0, d_model // tall, unroll=2 if d_model // tall % 2 == 0 else 1)
    def _(b):
        top = pl.multiple_of(b * tall, tall)
        there = pl.ds(top, tall)
        up = jnp.dot(xt[there, :], hg[...], preferred_element_type=F32)
        dn = jnp.dot(act[...], ct[:, there], preferred_element_type=F32)
        for i in range(0, tall, block):
            place = pl.ds(pl.multiple_of(top + i, block), block)
            which = b * (tall // block) + i // block
            for j in range(per):
                lanes = slice(j * block, (j + 1) * block)
                keep = keep_up[which, c * per + j].astype(F32)
                up_out[place, lanes] = (up[i:i + block, lanes] * keep).astype(BF16)
                keep = keep_dn[c * per + j, which].astype(F32)
                dn_out[lanes, place] = (dn[lanes, i:i + block] * keep).astype(BF16)


def body(rows, cols, inputs, up_weight, down_weight, up_mask, down_mask, cotangent):
    tokens, d_model = inputs.shape
    hidden = up_weight.shape[1]
    block = d_model // up_mask.shape[0]
    width = 2 * block if hidden % (2 * block) == 0 else block
    chunks = hidden // width
    halves = next(h for h in (4, 2, 1) if tokens % (h * cols * 16) == 0)
    tm = tokens // halves
    chips = cols // 2
    part = tm // cols
    slots = min(3 * halves, halves * chunks)
    vmem = pl.BlockSpec(memory_space=pltpu.VMEM)
    smem = pl.BlockSpec(memory_space=pltpu.SMEM)
    hbm = pl.BlockSpec(memory_space=pl.ANY)
    dma = pltpu.SemaphoreType.DMA
    sums, act, hg = pl.pallas_call(
        functools.partial(layer_kernel, rows, cols, halves, width, block, slots),
        out_shape=(
            jax.ShapeDtypeStruct((2, tokens, d_model), BF16),
            jax.ShapeDtypeStruct((hidden, tokens), BF16),
            jax.ShapeDtypeStruct((tokens, hidden), BF16),
        ),
        in_specs=[vmem, vmem, hbm, hbm, smem, smem],
        out_specs=(hbm, hbm, hbm),
        scratch_shapes=[
            pltpu.VMEM((chunks, d_model, width), BF16),
            pltpu.VMEM((chunks, width, d_model), BF16),
            pltpu.VMEM((halves, 2, tm, d_model), F32),
            pltpu.VMEM((slots, 2, tm, width), BF16),
            pltpu.VMEM((slots, 2, tm, width), BF16),
            pltpu.VMEM((slots, 2, tm, width), BF16),
            pltpu.VMEM((slots, width, tm), BF16),
            pltpu.VMEM((halves, 2, tm // 2, d_model), BF16),
            pltpu.VMEM((halves, 2, tm // 2, d_model), BF16),
            pltpu.VMEM((halves, chips, 2, part, d_model), BF16),
            pltpu.VMEM((halves, max(chips - 1, 1), 2, part, d_model), BF16),
            pltpu.VMEM((halves, 2, tm // 2, d_model), BF16),
            dma((2, chunks)),
            dma((slots,)), dma((slots,)), dma((slots,)), dma((slots,)),
            dma((2, slots)),
            pltpu.SemaphoreType.REGULAR, pltpu.SemaphoreType.REGULAR,
            dma((halves,)), dma((halves,)),
            dma((halves, max(chips - 1, 1))), dma((halves, max(chips - 1, 1))),
            dma((halves, max(chips - 1, 1))), dma((halves, max(chips - 1, 1))),
            dma((halves,)), dma((halves,)),
            dma((halves, 2)),
        ],
        compiler_params=pltpu.CompilerParams(collective_id=0, has_side_effects=True, vmem_limit_bytes=LIMIT),
        cost_estimate=pl.CostEstimate(
            flops=8 * tokens * d_model * hidden, bytes_accessed=4 * d_model * hidden, transcendentals=tokens * hidden),
    )(inputs, cotangent, up_weight, down_weight, up_mask, down_mask)

    wide = next(w for w in (4 * block, 2 * block, block) if hidden % w == 0)
    pieces = next(n for n in (4, 2, 1) if n <= hidden // wide and tokens % (n * 16) == 0)
    output, input_grad, up_grad, down_grad = pl.pallas_call(
        functools.partial(grads_kernel, block),
        grid=(hidden // wide,),
        out_shape=(
            jax.ShapeDtypeStruct((tokens, d_model), BF16),
            jax.ShapeDtypeStruct((tokens, d_model), BF16),
            jax.ShapeDtypeStruct((d_model, hidden), BF16),
            jax.ShapeDtypeStruct((hidden, d_model), BF16),
        ),
        in_specs=[
            pl.BlockSpec((tokens, d_model), lambda c: (0, 0)),
            pl.BlockSpec((tokens, d_model), lambda c: (0, 0)),
            pl.BlockSpec((wide, tokens), lambda c: (c, 0)),
            pl.BlockSpec((tokens, wide), lambda c: (0, c)),
            pl.BlockSpec((2, tokens // pieces, d_model), lambda c: (0, jnp.minimum(c, pieces - 1), 0)),
            smem, smem,
        ],
        out_specs=(
            pl.BlockSpec((tokens // pieces, d_model), lambda c: (jnp.minimum(c, pieces - 1), 0)),
            pl.BlockSpec((tokens // pieces, d_model), lambda c: (jnp.minimum(c, pieces - 1), 0)),
            pl.BlockSpec((d_model, wide), lambda c: (0, c)),
            pl.BlockSpec((wide, d_model), lambda c: (c, 0)),
        ),
        scratch_shapes=[pltpu.VMEM((d_model, tokens), BF16)],
        compiler_params=pltpu.CompilerParams(vmem_limit_bytes=LIMIT),
        cost_estimate=pl.CostEstimate(
            flops=4 * tokens * d_model * hidden, bytes_accessed=4 * d_model * hidden, transcendentals=0),
    )(inputs, cotangent, act, hg, sums, up_mask, down_mask)
    return (output, input_grad, up_grad, down_grad)


def solution(mesh):
    in_specs = (
        P(None, "row"),
        P("row", "col"),
        P("col", "row"),
        P("row", "col"),
        P("col", "row"),
        P(None, "row"),
    )
    out_specs = (P(None, "row"), P(None, "row"), P("row", "col"), P("col", "row"))
    step = functools.partial(body, mesh.shape["row"], mesh.shape["col"])
    return jax.shard_map(step, mesh=mesh, in_specs=in_specs, out_specs=out_specs, check_vma=False)
```
